32 devices in a mesh: angle: 4 (over y, core), tile: 8 (over z, x).
Axes of the slice: x: 2, y: 2, z: 4, core: 2. Of those that a mesh axis runs over, the one named last changes fastest.
Arguments:
- patches: bfloat16 [4, 64, 2, 128, 128], P('angle', 'tile'), may hold values from -6 to 6
- magnitudes: bfloat16 [4, 128, 128, 128], P('angle', 'tile'), may hold values from 0.099609375 to 3
- probe: float32 [2, 128, 128], replicated, may hold values from -6 to 6
- owners: int32 [4, 64, 1], P('angle', 'tile'), may hold values from 0 to 7; in each aligned block of 8 rows (0 to 7, 8 to 15, ..., all dimensions but the last counted through in order) at most 2 rows name the same one
- scan_rows: int32 [4, 64], P('angle', 'tile'), may hold values from 0 to 384
- scan_cols: int32 [4, 64], P('angle', 'tile'), may hold values from 0 to 896
- slab_rows: int32 [8, 4], P('tile'), may hold values from 0 to 32, as said below
- angle_tan: float32 [4], replicated, may hold values from -0.4 to 0.4
- prior_in: bfloat16 [16, 1, 3, 3], replicated, may hold values from -2 to 2
- prior_out: bfloat16 [1, 16, 3, 3], replicated, may hold values from -0.5 to 0.5
Outputs:
- volume: float32 [8, 128, 16, 1024], P('tile', 'angle')
The draws below stay inside these ranges and needn't reach their ends.
Inputs may be any that keep to these rules, and one draw needn't show every extreme that they name: `owners`: in the patches of one device, no owner is named by more than 2, and in some devices one owner is named exactly 2 times. Each row of slab_rows sums to 64, and in every row some slab has exactly 32 rows.
All inputs are finite; a program needn't handle non-finite values.
Results may differ from the reference program's by a relative error of at most 0.022.
Values may be sent and summed in bfloat16 or wider, within the bound.
No kernel may reach another device: no remote copies, remote signals or barrier semaphores. Data moves between devices by JAX's collectives and lax.ppermute only.
A program may use at most 128 MiB of HBM per device.

```python
import math
import jax
import jax.numpy as jnp
import numpy as np
from jax import lax

P_SIZE = 128
H = 512
W = 1024
CH = 16
PATCH_DEV = 8
XW = 16
ANGLES = 4
TILES = 8
CAP = 2
SLAB_MEAN = 16
ROWCAP = 32


def draw_slab_rows(key, part):
    half = ANGLES // 2
    first, second = jax.random.split(jax.random.fold_in(key, 17))
    delta = jax.random.randint(first, (TILES, half), -SLAB_MEAN, SLAB_MEAN + 1)
    picked = jax.random.randint(second, (TILES,), 0, half)
    delta = jnp.where(jnp.arange(half)[None, :] == picked[:, None], SLAB_MEAN, delta)
    counts = jnp.stack([SLAB_MEAN + delta, SLAB_MEAN - delta], axis=-1)
    return counts.reshape(TILES, ANGLES).astype(jnp.int32)


def set_ends(values, key, least, top_value):
    index_at = [jax.random.randint(jax.random.fold_in(key, axis), (), 0, length) for axis, length in enumerate(values.shape)]
    longest = values.shape.index(max(values.shape))
    beside = index_at[:longest] + [(index_at[longest] + 1) % values.shape[longest]] + index_at[longest + 1:]
    return values.at[tuple(index_at)].set(least).at[tuple(beside)].set(top_value)


def levels(rng, dims, cuts, low, top_value):
    gain = 1.0
    for dim, shards_of in cuts:
        heights = jax.random.uniform(jax.random.fold_in(jax.random.fold_in(rng, 6), dim), (shards_of,), jnp.float32, low / len(cuts), top_value / len(cuts))
        gain = gain * jnp.repeat(jnp.exp(heights), dims[dim] // shards_of).reshape((-1,) + (1,) * (len(dims) - 1 - dim))
    return gain


def assign_block(rng, own, number, rows, amount, top, most, skew):
    sequence = jax.random.permutation(rng, amount)
    packed, usual = portions_of(amount, rows * top, most, skew, True), portions_of(amount, rows * top, most, skew, False)
    places = jnp.arange(amount)

    def named(tallies, rotation):
        used = int((tallies > 0).sum())
        fixed = max(1, used // 4)
        moved = fixed + (places - fixed + rotation * (used - fixed)) % max(1, amount - fixed)
        return jnp.zeros((amount,), jnp.int32).at[sequence[jnp.where(places < fixed, places, moved)]].set(jnp.asarray(tallies, jnp.int32))

    tallies = jnp.where(number % 4 == 0, named(packed, number // 4), named(usual, number - number // 4 - 1))
    mixed = jax.random.permutation(jax.random.fold_in(own, 3), amount)
    giver, sink = mixed[0:amount // 2 * 2:2], mixed[1:amount // 2 * 2:2]
    slack = jnp.minimum(tallies[giver] - 1, most - tallies[sink]) // 2
    slack = jnp.where((giver == sequence[0]) | (sink == sequence[0]) | (tallies[sink] == 0), 0, jnp.maximum(slack, 0))
    moved = jax.random.randint(jax.random.fold_in(own, 4), (amount // 2,), 0, 1 << 20) % (slack + 1)
    tallies = tallies.at[giver].add(-moved).at[sink].add(moved)
    items = jnp.searchsorted(jnp.cumsum(tallies), jnp.arange(rows * top), side="right").astype(jnp.int32)
    grid = items.reshape(top, rows).T
    grid = grid[jax.random.permutation(jax.random.fold_in(own, 1), rows)]
    rotation = jax.random.randint(jax.random.fold_in(own, 2), (rows, 1), 0, top)
    return jnp.take_along_axis(grid, (jnp.arange(top)[None, :] + rotation) % top, axis=1)


def portions_of(number_of, total, limit, slope, full):
    loads = [(1 << 20) // math.isqrt(standing ** slope) + 1 for standing in range(1, number_of + 1)]
    largest = limit if full else min(limit, max(-(-total // number_of), total * loads[0] // sum(loads)))
    least = 1 if total - largest >= number_of - 1 else 0
    given, rest = [largest] + [least] * (number_of - 1), total - largest - least * (number_of - 1)
    while rest > 0:
        movable = [i for i in range(1, number_of) if given[i] < largest] or [i for i in range(1, number_of) if given[i] < limit]
        mass, budget = sum([loads[i] for i in movable]), rest
        for i in movable:
            addition = min(limit - given[i], max(1, budget * loads[i] // mass), rest)
            given[i] = given[i] + addition
            rest = rest - addition
    return np.array(given)


def gaussian(key, shape, spread, limit, cuts=(), held_as=jnp.bfloat16):
    gain = levels(key, shape, cuts, -0.22, 0.18) if cuts else 1.0
    array = jax.random.normal(key, shape, jnp.float32) * spread * gain
    return jnp.minimum(jnp.maximum(array, -limit), limit).astype(held_as)


def setup_inputs(seed: int = 0) -> dict:
    seeds = jax.random.split(jax.random.key(seed), 11)
    patches = gaussian(seeds[0], (ANGLES, TILES * PATCH_DEV, 2, P_SIZE, P_SIZE), 1.0, 6.0, ((0, 4), (1, 8)))
    magnitudes = jnp.clip(jnp.exp(math.log(3.0) - 3.4051113 * jax.random.uniform(seeds[1], (ANGLES, TILES * TILES * CAP, P_SIZE, P_SIZE), jnp.float32) ** levels(seeds[1], (ANGLES, TILES * TILES * CAP, P_SIZE, P_SIZE), ((0, 4), (1, 8)), -0.2, 0.2)), 0.099609375, 3.0).astype(jnp.bfloat16)
    probe = gaussian(seeds[2], (2, P_SIZE, P_SIZE), 1.0, 6.0, (), jnp.float32)
    owners_keys = jax.random.split(jax.random.fold_in(seeds[3], 1), ANGLES * (TILES * PATCH_DEV) // PATCH_DEV)
    owners_turns = jax.random.permutation(jax.random.fold_in(seeds[3], 3), ANGLES * (TILES * PATCH_DEV) // PATCH_DEV)
    owners = jax.vmap(lambda own, number: assign_block(jax.random.fold_in(seeds[3], 2), own, number, PATCH_DEV, TILES, 1, CAP, 1))(owners_keys, owners_turns).reshape((ANGLES, TILES * PATCH_DEV, 1))
    scan_rows = set_ends(jax.random.randint(seeds[4], (ANGLES, TILES * PATCH_DEV), 0, H - P_SIZE + 1), jax.random.fold_in(seeds[4], 1), 0, H - P_SIZE).astype(jnp.int32)
    scan_cols = set_ends(jax.random.randint(seeds[5], (ANGLES, TILES * PATCH_DEV), 0, W - P_SIZE + 1), jax.random.fold_in(seeds[5], 1), 0, W - P_SIZE).astype(jnp.int32)
    slab_rows = draw_slab_rows(jax.random.fold_in(seeds[10], 71), 0)
    angle_tan = jnp.clip(jax.random.uniform(seeds[7], (ANGLES,), jnp.float32, -0.4, 0.4), -0.4, 0.4)
    prior_in = gaussian(seeds[8], (CH, 1, 3, 3), 9 ** -0.5, 2.0)
    prior_out = gaussian(seeds[9], (1, CH, 3, 3), (9 * CH) ** -0.5, 0.5)
    return dict(patches=patches, magnitudes=magnitudes, probe=probe, owners=owners, scan_rows=scan_rows, scan_cols=scan_cols, slab_rows=slab_rows, angle_tan=angle_tan, prior_in=prior_in, prior_out=prior_out)


def dft_table(side):
    index = jnp.arange(side, dtype=jnp.int32)
    product = index[:, None] * index[None, :] % side
    phase = product.astype(jnp.float32) * (2.0 * math.pi / side)
    scale = 1.0 / math.sqrt(side)
    real = jnp.cos(phase) * scale
    imag = -jnp.sin(phase) * scale
    upper = jnp.concatenate([real, imag], axis=1)
    lower = jnp.concatenate([-imag, real], axis=1)
    return jnp.concatenate([upper, lower], axis=0).astype(jnp.bfloat16)

def correct_one(wave, measured, table):
    side = wave.shape[1]
    left = table.T
    joined = jnp.concatenate([wave[0], wave[1]], axis=1)
    half = jnp.dot(joined, table, preferred_element_type=jnp.float32).astype(jnp.bfloat16)
    stacked = jnp.concatenate([half[:, :side], half[:, side:]], axis=0)
    spectrum = jnp.dot(left, stacked, preferred_element_type=jnp.float32)
    real_part = spectrum[:side]
    imag_part = spectrum[side:]
    factor = measured.astype(jnp.float32) / jnp.sqrt(real_part * real_part + imag_part * imag_part + 0.25)
    target = jnp.concatenate([real_part * factor, imag_part * factor], axis=1).astype(jnp.bfloat16)
    back = jnp.dot(target, left, preferred_element_type=jnp.float32).astype(jnp.bfloat16)
    stacked_back = jnp.concatenate([back[:, :side], back[:, side:]], axis=0)
    result = jnp.dot(table, stacked_back, preferred_element_type=jnp.float32)
    return jnp.stack([result[:side], result[side:]], axis=0).astype(jnp.bfloat16)

def backproject(sino, angle_tan):
    count = sino.shape[1]
    offsets = jnp.arange(XW, dtype=jnp.float32) - (XW - 1) / 2.0
    columns = jnp.arange(W, dtype=jnp.float32)

    def add_angle(total, item):
        rows, tangent = item
        where = columns[None, :] + offsets[:, None] * tangent
        lower = jnp.floor(where)
        frac = where - lower
        low_index = lower.astype(jnp.int32)
        high_index = low_index + 1
        low_ok = ((low_index >= 0) & (low_index < W)).astype(jnp.float32)
        high_ok = ((high_index >= 0) & (high_index < W)).astype(jnp.float32)
        low_val = jnp.take(rows, jnp.clip(low_index, 0, W - 1), axis=1) * low_ok
        high_val = jnp.take(rows, jnp.clip(high_index, 0, W - 1), axis=1) * high_ok
        return (total + (1.0 - frac) * low_val + frac * high_val, None)
    start = jnp.zeros((count, XW, W), jnp.float32)
    total, unused = lax.scan(add_angle, start, (sino, angle_tan))
    return total / sino.shape[0]

def prior(slices, prior_in, prior_out):
    numbers = ('NCHW', 'OIHW', 'NCHW')
    rounded = slices.astype(jnp.bfloat16)[:, None].astype(jnp.float32)
    hidden = lax.conv_general_dilated(rounded, prior_in.astype(jnp.float32), (1, 1), 'SAME', dimension_numbers=numbers)
    hidden = jnp.maximum(hidden, 0.0).astype(jnp.bfloat16).astype(jnp.float32)
    extra = lax.conv_general_dilated(hidden, prior_out.astype(jnp.float32), (1, 1), 'SAME', dimension_numbers=numbers)
    return slices + extra[:, 0]

def reference(patches, magnitudes, probe, owners, scan_rows, scan_cols, slab_rows, angle_tan, prior_in, prior_out):
    table = dft_table(P_SIZE)
    sources = jnp.arange(TILES, dtype=jnp.int32)

    def one_angle(item):
        waves, stored, owner_all, rows_all, cols_all = item
        owner = owner_all[:, 0].reshape(TILES, PATCH_DEV)
        member = (owner[:, :, None] == sources[None, None, :]).astype(jnp.int32)
        rank = lax.optimization_barrier(jnp.sum((jnp.cumsum(member, axis=1) - member) * member, axis=2))
        index = (owner * (TILES * CAP) + sources[:, None] * CAP + rank).reshape(-1)
        measured = stored[index]
        fixed = lax.map(lambda pair: correct_one(pair[0], pair[1], table), (waves, measured))
        fixed = fixed.astype(jnp.float32)
        contrib = (probe[0] * fixed[:, 1] - probe[1] * fixed[:, 0]) * 0.25

        def place(step, canvas):
            row = rows_all[step]
            col = cols_all[step]
            piece = lax.dynamic_slice(canvas, (row, col), (P_SIZE, P_SIZE)) + contrib[step]
            return lax.dynamic_update_slice(canvas, piece, (row, col))
        return lax.fori_loop(0, waves.shape[0], place, jnp.zeros((H, W), jnp.float32))
    projection = lax.map(one_angle, (patches, magnitudes, owners, scan_rows, scan_cols))
    strip_rows = H // TILES
    strips = projection.reshape(ANGLES, TILES, strip_rows, W)
    starts = jnp.cumsum(slab_rows, axis=1) - slab_rows
    within = jnp.arange(ROWCAP, dtype=jnp.int32)

    def one_strip(item):
        strip, start, count = item
        index = jnp.clip(start[:, None] + within[None, :], 0, strip_rows - 1)
        valid = (within[None, :] < count[:, None]).astype(jnp.float32)
        picked = strip[:, index] * valid[None, :, :, None]

        def one_slab(slab):
            return prior(backproject(slab, angle_tan), prior_in, prior_out)
        slabs = lax.map(one_slab, jnp.moveaxis(picked, 1, 0))
        return slabs.reshape(ANGLES * ROWCAP, XW, W)
    return lax.map(one_strip, (jnp.moveaxis(strips, 1, 0), starts, slab_rows))
```

```python
import functools

import jax
import jax.numpy as jnp
import numpy as np
from jax import lax
from jax.experimental import pallas as pl
from jax.experimental.pallas import tpu as pltpu
from jax.sharding import PartitionSpec as P

H = 512
W = 1024
XW = 16
LANES = 128
SUBLANES = 8
PACK = 16
BEND = 3
REACH = BEND + 1
EDGE = BEND
TILE = 256
PAIR = 2
VMEM_LIMIT = 24 * 1024 * 1024


def dft_table(side):
    index = np.arange(side)
    phase = (index[:, None] * index[None, :] % side).astype(np.float64) * (2.0 * np.pi / side)
    scale = 1.0 / np.sqrt(side)
    real = np.cos(phase) * scale
    imag = -np.sin(phase) * scale
    table = np.block([[real, imag], [-imag, real]]).astype(np.float32)
    return jnp.asarray(table.astype(jnp.bfloat16))


def dot(left, right, precision=None):
    return jnp.dot(left, right, preferred_element_type=jnp.float32, precision=precision)


def swap_halves(values, pair, side):
    return jnp.concatenate(
        [
            jnp.concatenate(
                [values[k * side : (k + 1) * side, h * side : (h + 1) * side] for k in range(pair)], axis=1
            )
            for h in range(2)
        ],
        axis=0,
    )


def ahead(axis, step, size):
    return lax.rem(lax.axis_index(axis) + step, size)


def behind(axis, step, size):
    return lax.rem(lax.axis_index(axis) + (size - step), size)


def rotate(values, axis, size):
    ring = len(values)
    return [values[0]] + [
        lax.ppermute(values[step], axis, [(a, a // ring * ring + (a + step) % ring) for a in range(size)])
        for step in range(1, ring)
    ]


def deal_kernel(tiles, frames_ref, *refs):
    sources, out_refs, targets, sems = refs[:3], refs[3 : 3 + tiles], refs[3 + tiles : 6 + tiles], refs[-1]
    depth = out_refs[0].shape[0]
    copies = [
        pltpu.make_async_copy(
            frames_ref.at[pl.ds(ahead("tile", step, tiles) * depth, depth)], out_refs[step], sems.at[step]
        )
        for step in range(tiles)
    ]
    copies += [
        pltpu.make_async_copy(source, target, sems.at[tiles + k])
        for k, (source, target) in enumerate(zip(sources, targets))
    ]
    for copy in copies:
        copy.start()
    for copy in copies:
        copy.wait()


def deal(frames, tiles, *others):
    depth = frames.shape[0] // tiles
    results = pl.pallas_call(
        functools.partial(deal_kernel, tiles),
        out_shape=(pltpu.VMEM((depth,) + frames.shape[1:], frames.dtype),) * tiles
        + tuple(pltpu.VMEM(x.shape, x.dtype) for x in others),
        in_specs=[pl.BlockSpec(memory_space=pltpu.HBM)] * (1 + len(others)),
        out_specs=(pl.BlockSpec(memory_space=pltpu.VMEM),) * (tiles + len(others)),
        scratch_shapes=[pltpu.SemaphoreType.DMA((tiles + len(others),))],
        compiler_params=pltpu.CompilerParams(vmem_limit_bytes=VMEM_LIMIT),
        name="deal",
    )(*[pltpu.with_memory_space_constraint(x, pltpu.HBM) for x in (frames, *others)])
    return list(results[:tiles]), *results[tiles:]


def turned_table(table):
    side = table.shape[0] // 2
    return jnp.concatenate(
        [
            jnp.concatenate([table[:side, :side], table[side:, :side]], axis=1),
            jnp.concatenate([table[:side, side:], table[side:, side:]], axis=1),
        ],
        axis=0,
    )


def prepare_kernel(patch_ref, table_ref, unit_ref):
    count, _, side, _ = patch_ref.shape
    table = table_ref[...]
    left = turned_table(table)
    for first in range(0, count, PAIR):
        joined = jnp.concatenate(
            [jnp.concatenate([patch_ref[k, 0], patch_ref[k, 1]], axis=1) for k in range(first, first + PAIR)],
            axis=0,
        )
        half = dot(joined, table).astype(jnp.bfloat16)
        spectrum = dot(left, swap_halves(half, PAIR, side))
        real = spectrum[:side]
        imag = spectrum[side:]
        factor = lax.rsqrt(real * real + imag * imag + 0.25)
        cut = slice(first * side, (first + PAIR) * side)
        unit_ref[:side, cut] = real * factor
        unit_ref[side:, cut] = imag * factor


def prepare(waves, table):
    count, _, side, _ = waves.shape
    vmem = pl.BlockSpec(memory_space=pltpu.VMEM)
    return pl.pallas_call(
        prepare_kernel,
        out_shape=pltpu.VMEM((2 * side, count * side), jnp.float32),
        in_specs=[vmem] * 2,
        out_specs=vmem,
        compiler_params=pltpu.CompilerParams(vmem_limit_bytes=VMEM_LIMIT),
        name="prepare",
    )(waves, table)


def project_kernel(tiles, place_ref, unit_ref, probe_ref, table_ref, *refs):
    level_refs, out_refs = refs[:tiles], refs[tiles : 2 * tiles]
    canvas, levels = refs[2 * tiles :]
    depth, side = level_refs[0].shape[:2]
    count = unit_ref.shape[1] // side
    for step, level_ref in enumerate(level_refs):
        levels[step * depth : (step + 1) * depth] = level_ref[...]
    owner = [place_ref[0, k] for k in range(count)]
    slots = []
    for k in range(count):
        rank = jnp.int32(0)
        for j in range(k):
            rank = rank + jnp.where(owner[j] == owner[k], 1, 0)
        slots.append(behind("tile", owner[k], tiles) * depth + rank)
    table = table_ref[...]
    left = turned_table(table)
    canvas[...] = jnp.zeros_like(canvas)
    tall = side + SUBLANES
    lane = lax.broadcasted_iota(jnp.int32, (tall, side), 1)
    for first in range(0, count, PAIR):
        level = [levels[slots[k]].astype(jnp.float32) for k in range(first, first + PAIR)]
        level = jnp.concatenate(level, axis=1)
        cut = slice(first * side, (first + PAIR) * side)
        real = (unit_ref[:side, cut] * level).astype(jnp.bfloat16)
        imag = (unit_ref[side:, cut] * level).astype(jnp.bfloat16)
        target = jnp.concatenate(
            [
                jnp.concatenate([real[:, k * side : (k + 1) * side], imag[:, k * side : (k + 1) * side]], axis=1)
                for k in range(PAIR)
            ],
            axis=0,
        )
        back = dot(target, left).astype(jnp.bfloat16)
        result = dot(table, swap_halves(back, PAIR, side))
        for k in range(PAIR):
            fixed_re = result[:side, k * side : (k + 1) * side]
            fixed_im = result[side:, k * side : (k + 1) * side]
            contrib = probe_ref[0] * fixed_im - probe_ref[1] * fixed_re
            row = place_ref[1, first + k]
            col = place_ref[2, first + k]
            down = lax.rem(row, SUBLANES)
            shift = lax.rem(col, LANES)
            top = pl.multiple_of(row - down, SUBLANES)
            base = pl.multiple_of(col - shift, LANES)
            turned = jnp.concatenate([contrib, jnp.zeros((SUBLANES, side), jnp.float32)], axis=0)
            turned = pltpu.roll(pltpu.roll(turned, down, 0), shift, 1)
            piece = jnp.concatenate(
                [jnp.where(lane >= shift, turned, 0.0), jnp.where(lane < shift, turned, 0.0)], axis=1
            )
            where = (pl.ds(top, tall), pl.ds(base, 2 * side))
            canvas[where] = canvas[where] + piece
    strip_rows, width = out_refs[0].shape
    half = tiles // 2
    me = lax.axis_index("tile")
    place = lax.rem(me, half)
    for step in range(half):
        turn = lax.rem(place + step, half)
        near = pl.multiple_of((me - place + turn) * strip_rows, strip_rows)
        far = pl.multiple_of((half - (me - place) + turn) * strip_rows, strip_rows)
        out_refs[step][...] = canvas[pl.ds(near, strip_rows), :width].astype(jnp.bfloat16)
        out_refs[half + step][...] = canvas[pl.ds(far, strip_rows), :width].astype(jnp.bfloat16)


def project(place, unit, probe, table, levels):
    tiles = len(levels)
    depth, side = levels[0].shape[:2]
    smem = pl.BlockSpec(memory_space=pltpu.SMEM)
    vmem = pl.BlockSpec(memory_space=pltpu.VMEM)
    return pl.pallas_call(
        functools.partial(project_kernel, tiles),
        out_shape=(jax.ShapeDtypeStruct((H // tiles, W), jnp.bfloat16),) * tiles,
        in_specs=[smem] + [vmem] * (3 + tiles),
        out_specs=(vmem,) * tiles,
        scratch_shapes=[
            pltpu.VMEM((H + SUBLANES, W + side), jnp.float32),
            pltpu.VMEM((tiles * depth, side, side), levels[0].dtype),
        ],
        compiler_params=pltpu.CompilerParams(vmem_limit_bytes=VMEM_LIMIT),
        name="project",
    )(place, unit, probe, table, *levels)


def slabs_kernel(count, select_ref, *refs):
    strips = jnp.concatenate([ref[...] for ref in refs[:count]], axis=0)
    result = dot(select_ref[...], strips).astype(jnp.bfloat16)
    rowcap = refs[count].shape[0]
    for step, out_ref in enumerate(refs[count:]):
        out_ref[...] = result[step * rowcap : (step + 1) * rowcap]


def cut_slabs(select, strips, angles):
    rowcap = select.shape[0] // angles
    vmem = pl.BlockSpec(memory_space=pltpu.VMEM)
    return pl.pallas_call(
        functools.partial(slabs_kernel, len(strips)),
        out_shape=(jax.ShapeDtypeStruct((rowcap, strips[0].shape[1]), jnp.bfloat16),) * angles,
        in_specs=[vmem] * (1 + len(strips)),
        out_specs=(vmem,) * angles,
        compiler_params=pltpu.CompilerParams(vmem_limit_bytes=VMEM_LIMIT),
        name="cut_slabs",
    )(select, *strips)


def selection(length_ref, shape, strip_rows):
    angles = length_ref.shape[0]
    rowcap = shape[0] // angles
    row = lax.broadcasted_iota(jnp.int32, shape, 0)
    source = lax.broadcasted_iota(jnp.int32, shape, 1) % strip_rows
    wanted = jnp.full(shape, -1, jnp.int32)
    for step in range(angles):
        slab = ahead("angle", step, angles)
        start = jnp.int32(0)
        for q in range(angles):
            start = start + jnp.where(q < slab, length_ref[q], 0)
        within = row - step * rowcap
        good = (within >= 0) & (within < rowcap) & (within < length_ref[slab])
        wanted = jnp.where(good, within + start, wanted)
    return jnp.where(source == wanted, 1.0, 0.0).astype(jnp.bfloat16)


def weights_kernel(strip_rows, tan_ref, length_ref, first_ref, second_ref, out_ref, last_ref, select_ref, order_ref):
    angles = tan_ref.shape[0]
    channels = first_ref.shape[0]
    group = PACK // angles
    wide = channels * XW
    steps = 2 * REACH + 1
    exact = lax.Precision.HIGHEST

    shape = (3 * XW, TILE)
    line = lax.broadcasted_iota(jnp.int32, shape, 0)
    column = lax.broadcasted_iota(jnp.int32, shape, 1)
    dj = line // XW - 1
    offset = (line % XW).astype(jnp.float32) - (XW - 1) / 2.0
    step = column // PACK
    tangent = jnp.zeros(shape, jnp.float32)
    for a in range(angles):
        source = behind("angle", a, angles)
        tangent = jnp.where(column % angles == a, tan_ref[source], tangent)
    shifted = jnp.clip(offset * tangent, -float(BEND), float(BEND))
    floor_shift = jnp.floor(shifted)
    fraction = shifted - floor_shift

    def share(at):
        at = at.astype(jnp.float32)
        low = jnp.where(at == floor_shift, 1.0 - fraction, 0.0)
        return (low + jnp.where(at == floor_shift + 1.0, fraction, 0.0)) * (0.25 / angles)

    position = step - steps
    shear = jnp.where(step < steps, share(step - REACH - dj), 0.0)
    on_left = (position >= 0) & (position < EDGE) & (dj == -1)
    on_right = (position >= EDGE) & (position < 2 * EDGE) & (dj == 1)
    shear = shear - jnp.where(on_left, share(position + 1), 0.0) - jnp.where(on_right, share(EDGE - 1 - position), 0.0)

    tall = (wide, 3 * XW)
    line = lax.broadcasted_iota(jnp.int32, tall, 0)
    column = lax.broadcasted_iota(jnp.int32, tall, 1)
    spread = lax.broadcasted_iota(jnp.int32, (wide, channels), 0) // XW
    spread = (spread == lax.broadcasted_iota(jnp.int32, (wide, channels), 1)).astype(jnp.float32)
    taps = dot(spread, first_ref[...].astype(jnp.float32), exact)
    band = jnp.zeros(tall, jnp.float32)
    for di in range(3):
        for at in range(3):
            hit = (column % XW - line % XW == di - 1) & (column // XW == at)
            band = band + jnp.where(hit, taps[:, 3 * di + at : 3 * di + at + 1], 0.0)

    slab_row = lax.broadcasted_iota(jnp.int32, (wide, TILE), 1) % PACK // angles
    flat_row = lax.broadcasted_iota(jnp.int32, (XW, TILE), 1) % PACK // angles
    mixed = dot(band, shear, exact)
    for r in range(group):
        out_ref[r * wide : (r + 1) * wide, :] = jnp.where(slab_row == r, mixed, 0.0).astype(jnp.bfloat16)
        out_ref[group * wide + r * XW : group * wide + (r + 1) * XW, :] = jnp.where(
            flat_row == r, shear[XW : 2 * XW], 0.0
        ).astype(jnp.bfloat16)

    gather = lax.broadcasted_iota(jnp.int32, (channels, wide), 1) // XW
    gather = (gather == lax.broadcasted_iota(jnp.int32, (channels, wide), 0)).astype(jnp.float32)
    taps = dot(second_ref[...].astype(jnp.float32), gather, exact)
    line = lax.broadcasted_iota(jnp.int32, (XW, wide), 0)
    column = lax.broadcasted_iota(jnp.int32, (XW, wide), 1) % XW
    for at in range(3):
        total = jnp.zeros((XW, wide), jnp.float32)
        for di in range(3):
            total = total + jnp.where(column - line == di - 1, taps[3 * di + at : 3 * di + at + 1, :], 0.0)
        last_ref[at * XW : (at + 1) * XW, :] = total.astype(jnp.bfloat16)


    select_ref[...] = selection(length_ref, select_ref.shape, strip_rows)
    rows = order_ref.shape[0]
    line = lax.broadcasted_iota(jnp.int32, (rows, rows), 0)
    source = lax.broadcasted_iota(jnp.int32, (rows, rows), 1)
    hit = source == line % angles * (rows // angles) + line // angles
    order_ref[...] = jnp.where(hit, 1.0, 0.0).astype(jnp.bfloat16)


def make_weights(angle_tan, lengths, prior_in, prior_out, strip_rows, parts):
    angles = angle_tan.shape[0]
    channels = prior_in.shape[0]
    rows = PACK // angles * XW * (channels + 1)
    smem = pl.BlockSpec(memory_space=pltpu.SMEM)
    vmem = pl.BlockSpec(memory_space=pltpu.VMEM)
    return pl.pallas_call(
        functools.partial(weights_kernel, strip_rows),
        out_shape=(
            pltpu.VMEM((rows, TILE), jnp.bfloat16),
            pltpu.VMEM((3 * XW, channels * XW), jnp.bfloat16),
            pltpu.VMEM((2 * strip_rows, parts * strip_rows), jnp.bfloat16),
            pltpu.VMEM((2 * strip_rows, 2 * strip_rows), jnp.bfloat16),
        ),
        in_specs=[smem, smem, vmem, vmem],
        out_specs=(vmem,) * 4,
        compiler_params=pltpu.CompilerParams(vmem_limit_bytes=VMEM_LIMIT),
        name="make_weights",
    )(angle_tan, lengths, prior_in.reshape(channels, 9), prior_out.reshape(channels, 9).T)


def slide(values, by, lane):
    if by == 0:
        return values
    width = values.shape[1]
    turned = pltpu.roll(values, (-by) % width, 1)
    return jnp.where((lane < width - by) if by > 0 else (lane >= -by), turned, 0.0)


def volume_kernel(*refs):
    *piece_refs, first_ref, last_ref, order_ref, out_ref, ordered, even, odd, held, sems = refs
    angles = len(piece_refs)
    rowcap, width = piece_refs[0].shape
    rows = angles * rowcap
    group = PACK // angles
    groups = rowcap // group
    wide = last_ref.shape[1]
    tiles = width // TILE
    span = 2 * REACH + 1

    ordered[...] = dot(order_ref[...], jnp.concatenate([ref[...] for ref in piece_refs], axis=0))

    lane = lax.broadcasted_iota(jnp.int32, (PACK, width), 1)
    inside = lax.broadcasted_iota(jnp.int32, (PACK, LANES), 1)

    def stack_rows(here, target):
        taken = ordered[pl.ds(pl.multiple_of(here * PACK, PACK), PACK), :]
        moved = {by: slide(taken, by, lane) for by in range(-REACH, REACH + 1)}
        for by, value in moved.items():
            at = (by + REACH) * PACK
            target[at : at + PACK, :] = value.astype(jnp.bfloat16)
        for q in range(EDGE):
            at = (span + q) * PACK
            target[at : at + PACK, :LANES] = jnp.where(inside == 0, moved[q][:, :LANES], 0.0).astype(jnp.bfloat16)
            at += EDGE * PACK
            target[at : at + PACK, width - LANES :] = jnp.where(
                inside == LANES - 1, moved[-q][:, width - LANES :], 0.0
            ).astype(jnp.bfloat16)

    def copy_out(here):
        part = pl.ds(here * group, group)
        return pltpu.make_async_copy(held.at[part], out_ref.at[part], sems.at[here])

    def one_group(here, stack):
        base = []
        partial = [[] for _ in range(group)]
        waiting = None
        for n in range(tiles + 1):
            hidden = None
            if n < tiles:
                mixed = dot(first_ref[...], stack[:, n * TILE : (n + 1) * TILE])
                base.append(mixed[group * wide :])
                hidden = jnp.maximum(mixed[: group * wide].astype(jnp.bfloat16), 0.0)
            if waiting is not None:
                for r in range(group):
                    partial[r].append(dot(last_ref[...], waiting[r * wide : (r + 1) * wide]))
            waiting = hidden
        base = jnp.concatenate(base, axis=1)
        for r in range(group):
            sums = jnp.concatenate(partial[r], axis=1)
            held[here * group + r] = (
                base[r * XW : (r + 1) * XW]
                + sums[XW : 2 * XW]
                + slide(sums[:XW], -1, lane)
                + slide(sums[2 * XW :], 1, lane)
            )
        copy_out(here).start()

    even[span * PACK :, :] = jnp.zeros((TILE - span * PACK, width), jnp.bfloat16)
    odd[span * PACK :, :] = jnp.zeros((TILE - span * PACK, width), jnp.bfloat16)
    stack_rows(0, even)

    def two_groups(step, carry):
        here = 2 * step
        stack_rows(here + 1, odd)
        one_group(here, even)
        stack_rows(lax.rem(here + 2, groups), even)
        one_group(here + 1, odd)
        return carry

    lax.fori_loop(0, groups // 2, two_groups, 0)

    def finish(here, carry):
        copy_out(here).wait()
        return carry

    lax.fori_loop(0, groups, finish, 0)


def make_volume(pieces, first, last, order):
    angles = len(pieces)
    rowcap, width = pieces[0].shape
    vmem = pl.BlockSpec(memory_space=pltpu.VMEM)
    shape = (rowcap, XW, width)
    return pl.pallas_call(
        volume_kernel,
        out_shape=jax.ShapeDtypeStruct(shape, jnp.float32),
        in_specs=[vmem] * (angles + 3),
        out_specs=pl.BlockSpec(memory_space=pl.ANY),
        scratch_shapes=[
            pltpu.VMEM((angles * rowcap, width), jnp.float32),
            pltpu.VMEM((TILE, width), jnp.bfloat16),
            pltpu.VMEM((TILE, width), jnp.bfloat16),
            pltpu.VMEM(shape, jnp.float32),
            pltpu.SemaphoreType.DMA((rowcap * angles // PACK,)),
        ],
        compiler_params=pltpu.CompilerParams(vmem_limit_bytes=VMEM_LIMIT),
        name="make_volume",
    )(*pieces, first, last, order)


def body(
    patches,
    magnitudes,
    probe,
    owners,
    scan_rows,
    scan_cols,
    slab_rows,
    angle_tan,
    prior_in,
    prior_out,
):
    tiles = lax.axis_size("tile")
    angles = lax.axis_size("angle")
    half = tiles // 2
    levels, waves, probe, table = deal(magnitudes[0], tiles, patches[0], probe, dft_table(patches.shape[3]))
    levels = rotate(levels, "tile", tiles)
    place = jnp.stack([owners[0, :, 0], scan_rows[0], scan_cols[0]])
    waves, levels[1], levels[-1] = lax.optimization_barrier((waves, levels[1], levels[-1]))
    strips = project(place, prepare(waves, table), probe, table, levels)
    near, far = strips[:half], strips[half:]
    angle_tan, prior_in, prior_out, unused = lax.optimization_barrier(
        (angle_tan, prior_in, prior_out, near[0])
    )
    first, last, select, order = make_weights(
        angle_tan, slab_rows[0], prior_in, prior_out, H // tiles, half + 1
    )
    far = rotate(far, "tile", tiles)
    far = sum(part.astype(jnp.float32) for part in far).astype(jnp.bfloat16)
    far, *near = lax.optimization_barrier((far, *near))
    far = lax.ppermute(far, "tile", [(a, (a + half) % tiles) for a in range(tiles)])
    near = rotate(near, "tile", tiles)
    select, near[0] = lax.optimization_barrier((select, near[0]))
    slabs = cut_slabs(select, [far] + near, angles)
    return make_volume(rotate(slabs, "angle", angles), first, last, order)[None]


def solution(mesh):
    placed = (
        P("angle", "tile", None, None, None),
        P("angle", "tile", None, None),
        P(),
        P("angle", "tile", None),
        P("angle", "tile"),
        P("angle", "tile"),
        P("tile", None),
        P(),
        P(),
        P(),
    )
    return jax.shard_map(
        body, mesh=mesh, in_specs=placed, out_specs=P("tile", "angle", None, None), check_vma=False
    )
```

```python
import functools

import jax
import jax.numpy as jnp
import numpy as np
from jax import lax
from jax.experimental import pallas as pl
from jax.experimental.pallas import tpu as pltpu
from jax.sharding import PartitionSpec as P

H = 512
W = 1024
XW = 16
LANES = 128
SUBLANES = 8
PACK = 16
BEND = 3
REACH = BEND + 1
EDGE = BEND
TILE = 256
PAIR = 4
VMEM_LIMIT = 24 * 1024 * 1024


def dft_table(side):
    index = np.arange(side)
    phase = (index[:, None] * index[None, :] % side).astype(np.float64) * (2.0 * np.pi / side)
    scale = 1.0 / np.sqrt(side)
    real = np.cos(phase) * scale
    imag = -np.sin(phase) * scale
    table = np.block([[real, imag], [-imag, real]]).astype(np.float32)
    return jnp.asarray(table.astype(jnp.bfloat16))


def dot(left, right, precision=None):
    return jnp.dot(left, right, preferred_element_type=jnp.float32, precision=precision)


def swap_halves(values, pair, side):
    return jnp.concatenate(
        [
            jnp.concatenate(
                [values[k * side : (k + 1) * side, h * side : (h + 1) * side] for k in range(pair)], axis=1
            )
            for h in range(2)
        ],
        axis=0,
    )


def ahead(axis, step, size):
    return lax.rem(lax.axis_index(axis) + step, size)


def behind(axis, step, size):
    return lax.rem(lax.axis_index(axis) + (size - step), size)


def sending_order(size):
    load = sorted(range(1, size), key=lambda step: abs(2 * step - size))
    return [0, load[0], 1, size - 1] + [step for step in load[1:] if step not in (1, size - 1)]


def rotate(values, axis):
    size = len(values)
    return [values[0]] + [
        lax.ppermute(values[step], axis, [(a, (a + step) % size) for a in range(size)])
        for step in range(1, size)
    ]


def swap(value, axis, step, size):
    return lax.ppermute(value, axis, [(a, a ^ step) for a in range(size)])


def deal_kernel(frames_ref, *refs):
    *out_refs, sems = refs
    tiles = len(out_refs)
    depth = out_refs[0].shape[0]
    copies = [
        pltpu.make_async_copy(
            frames_ref.at[pl.ds(ahead("tile", step, tiles) * depth, depth)], out_refs[step], sems.at[step]
        )
        for step in range(tiles)
    ]
    for copy in copies:
        copy.start()
    for copy in copies:
        copy.wait()


def deal(frames, tiles):
    depth = frames.shape[0] // tiles
    return pl.pallas_call(
        deal_kernel,
        out_shape=(jax.ShapeDtypeStruct((depth,) + frames.shape[1:], frames.dtype),) * tiles,
        in_specs=[pl.BlockSpec(memory_space=pltpu.HBM)],
        out_specs=(pl.BlockSpec(memory_space=pltpu.VMEM),) * tiles,
        scratch_shapes=[pltpu.SemaphoreType.DMA((tiles,))],
        compiler_params=pltpu.CompilerParams(vmem_limit_bytes=VMEM_LIMIT),
        name="deal",
    )(pltpu.with_memory_space_constraint(frames, pltpu.HBM))


def turned_table(table):
    side = table.shape[0] // 2
    return jnp.concatenate(
        [
            jnp.concatenate([table[:side, :side], table[side:, :side]], axis=1),
            jnp.concatenate([table[:side, side:], table[side:, side:]], axis=1),
        ],
        axis=0,
    )


def prepare_kernel(patch_hbm, probe_hbm, table_hbm, unit_ref, probe_ref, table_ref, patch_ref, sems):
    count, _, side, _ = patch_ref.shape
    steps = count // PAIR
    small = [
        pltpu.make_async_copy(source, target, sems.at[steps + k])
        for k, (source, target) in enumerate(((table_hbm, table_ref), (probe_hbm, probe_ref)))
    ]
    large = [
        pltpu.make_async_copy(
            patch_hbm.at[pl.ds(k * PAIR, PAIR)], patch_ref.at[pl.ds(k * PAIR, PAIR)], sems.at[k]
        )
        for k in range(steps)
    ]
    for copy in small[:1] + large + small[1:]:
        copy.start()
    small[0].wait()
    table = table_ref[...]
    left = turned_table(table)
    for step in range(steps):
        large[step].wait()
        first = step * PAIR
        joined = jnp.concatenate(
            [jnp.concatenate([patch_ref[k, 0], patch_ref[k, 1]], axis=1) for k in range(first, first + PAIR)],
            axis=0,
        )
        half = dot(joined, table).astype(jnp.bfloat16)
        spectrum = dot(left, swap_halves(half, PAIR, side))
        real = spectrum[:side]
        imag = spectrum[side:]
        factor = lax.rsqrt(real * real + imag * imag + 0.25)
        cut = slice(first * side, (first + PAIR) * side)
        unit_ref[:side, cut] = real * factor
        unit_ref[side:, cut] = imag * factor
    small[1].wait()


def prepare(waves, probe):
    count, _, side, _ = waves.shape
    hbm = pl.BlockSpec(memory_space=pltpu.HBM)
    vmem = pl.BlockSpec(memory_space=pltpu.VMEM)
    return pl.pallas_call(
        prepare_kernel,
        out_shape=(
            pltpu.VMEM((2 * side, count * side), jnp.float32),
            pltpu.VMEM(probe.shape, jnp.float32),
            pltpu.VMEM((2 * side, 2 * side), jnp.bfloat16),
        ),
        in_specs=[hbm] * 3,
        out_specs=(vmem,) * 3,
        scratch_shapes=[
            pltpu.VMEM(waves.shape, waves.dtype),
            pltpu.SemaphoreType.DMA((count // PAIR + 2,)),
        ],
        compiler_params=pltpu.CompilerParams(vmem_limit_bytes=VMEM_LIMIT),
        name="prepare",
    )(*[pltpu.with_memory_space_constraint(x, pltpu.HBM) for x in (waves, probe, dft_table(side))])


def project_kernel(tiles, place_ref, unit_ref, probe_ref, table_ref, *refs):
    level_refs, out_refs = refs[:tiles], refs[tiles : 2 * tiles]
    canvas, levels = refs[2 * tiles :]
    depth, side = level_refs[0].shape[:2]
    count = unit_ref.shape[1] // side
    for step, level_ref in zip(sending_order(tiles), level_refs):
        levels[step * depth : (step + 1) * depth] = level_ref[...]
    owner = [place_ref[0, k] for k in range(count)]
    slots = []
    for k in range(count):
        rank = jnp.int32(0)
        for j in range(k):
            rank = rank + jnp.where(owner[j] == owner[k], 1, 0)
        slots.append(behind("tile", owner[k], tiles) * depth + rank)
    table = table_ref[...]
    left = turned_table(table)
    canvas[...] = jnp.zeros_like(canvas)
    tall = side + SUBLANES
    lane = lax.broadcasted_iota(jnp.int32, (tall, side), 1)
    for first in range(0, count, PAIR):
        level = [levels[slots[k]].astype(jnp.float32) for k in range(first, first + PAIR)]
        level = jnp.concatenate(level, axis=1)
        cut = slice(first * side, (first + PAIR) * side)
        real = (unit_ref[:side, cut] * level).astype(jnp.bfloat16)
        imag = (unit_ref[side:, cut] * level).astype(jnp.bfloat16)
        target = jnp.concatenate(
            [
                jnp.concatenate([real[:, k * side : (k + 1) * side], imag[:, k * side : (k + 1) * side]], axis=1)
                for k in range(PAIR)
            ],
            axis=0,
        )
        back = dot(target, left).astype(jnp.bfloat16)
        result = dot(table, swap_halves(back, PAIR, side))
        for k in range(PAIR):
            fixed_re = result[:side, k * side : (k + 1) * side]
            fixed_im = result[side:, k * side : (k + 1) * side]
            contrib = probe_ref[0] * fixed_im - probe_ref[1] * fixed_re
            row = place_ref[1, first + k]
            col = place_ref[2, first + k]
            down = lax.rem(row, SUBLANES)
            shift = lax.rem(col, LANES)
            top = pl.multiple_of(row - down, SUBLANES)
            base = pl.multiple_of(col - shift, LANES)
            turned = jnp.concatenate([contrib, jnp.zeros((SUBLANES, side), jnp.float32)], axis=0)
            turned = pltpu.roll(pltpu.roll(turned, down, 0), shift, 1)
            piece = jnp.concatenate(
                [jnp.where(lane >= shift, turned, 0.0), jnp.where(lane < shift, turned, 0.0)], axis=1
            )
            where = (pl.ds(top, tall), pl.ds(base, 2 * side))
            canvas[where] = canvas[where] + piece
    strip_rows, width = out_refs[0].shape
    me = lax.axis_index("tile")
    for step in range(tiles):
        top = pl.multiple_of(lax.bitwise_xor(me, jnp.int32(step)) * strip_rows, strip_rows)
        out_refs[step][...] = canvas[pl.ds(top, strip_rows), :width].astype(jnp.bfloat16)


def project(place, unit, probe, table, levels):
    tiles = len(levels)
    depth, side = levels[0].shape[:2]
    smem = pl.BlockSpec(memory_space=pltpu.SMEM)
    vmem = pl.BlockSpec(memory_space=pltpu.VMEM)
    return pl.pallas_call(
        functools.partial(project_kernel, tiles),
        out_shape=(jax.ShapeDtypeStruct((H // tiles, W), jnp.bfloat16),) * tiles,
        in_specs=[smem] + [vmem] * (3 + tiles),
        out_specs=(vmem,) * tiles,
        scratch_shapes=[
            pltpu.VMEM((H + SUBLANES, W + side), jnp.float32),
            pltpu.VMEM((tiles * depth, side, side), levels[0].dtype),
        ],
        compiler_params=pltpu.CompilerParams(vmem_limit_bytes=VMEM_LIMIT),
        name="project",
    )(place, unit, probe, table, *levels)


def slabs_kernel(count, select_ref, *refs):
    strips = jnp.concatenate([ref[...] for ref in refs[:count]], axis=0)
    result = dot(select_ref[...], strips).astype(jnp.bfloat16)
    rowcap = refs[count].shape[0]
    for step, out_ref in enumerate(refs[count:]):
        out_ref[...] = result[step * rowcap : (step + 1) * rowcap]


def cut_slabs(select, strips, angles):
    rowcap = select.shape[0] // angles
    vmem = pl.BlockSpec(memory_space=pltpu.VMEM)
    return pl.pallas_call(
        functools.partial(slabs_kernel, len(strips)),
        out_shape=(jax.ShapeDtypeStruct((rowcap, strips[0].shape[1]), jnp.bfloat16),) * angles,
        in_specs=[vmem] * (1 + len(strips)),
        out_specs=(vmem,) * angles,
        compiler_params=pltpu.CompilerParams(vmem_limit_bytes=VMEM_LIMIT),
        name="cut_slabs",
    )(select, *strips)


def selection(length_ref, shape, strip_rows):
    angles = length_ref.shape[0]
    rowcap = shape[0] // angles
    row = lax.broadcasted_iota(jnp.int32, shape, 0)
    source = lax.broadcasted_iota(jnp.int32, shape, 1) % strip_rows
    wanted = jnp.full(shape, -1, jnp.int32)
    for step in range(angles):
        slab = ahead("angle", step, angles)
        start = jnp.int32(0)
        for q in range(angles):
            start = start + jnp.where(q < slab, length_ref[q], 0)
        within = row - step * rowcap
        good = (within >= 0) & (within < rowcap) & (within < length_ref[slab])
        wanted = jnp.where(good, within + start, wanted)
    return jnp.where(source == wanted, 1.0, 0.0).astype(jnp.bfloat16)


def weights_kernel(strip_rows, tan_ref, length_ref, first_ref, second_ref, out_ref, last_ref, select_ref, order_ref, filled_ref):
    angles = tan_ref.shape[0]
    channels = first_ref.shape[0]
    group = PACK // angles
    wide = channels * XW
    steps = 2 * REACH + 1
    exact = lax.Precision.HIGHEST

    shape = (3 * XW, TILE)
    line = lax.broadcasted_iota(jnp.int32, shape, 0)
    column = lax.broadcasted_iota(jnp.int32, shape, 1)
    dj = line // XW - 1
    offset = (line % XW).astype(jnp.float32) - (XW - 1) / 2.0
    step = column // PACK
    tangent = jnp.zeros(shape, jnp.float32)
    for a in range(angles):
        source = behind("angle", a, angles)
        tangent = jnp.where(column % angles == a, tan_ref[source], tangent)
    shifted = jnp.clip(offset * tangent, -float(BEND), float(BEND))
    floor_shift = jnp.floor(shifted)
    fraction = shifted - floor_shift

    def share(at):
        at = at.astype(jnp.float32)
        low = jnp.where(at == floor_shift, 1.0 - fraction, 0.0)
        return (low + jnp.where(at == floor_shift + 1.0, fraction, 0.0)) * (0.25 / angles)

    position = step - steps
    shear = jnp.where(step < steps, share(step - REACH - dj), 0.0)
    on_left = (position >= 0) & (position < EDGE) & (dj == -1)
    on_right = (position >= EDGE) & (position < 2 * EDGE) & (dj == 1)
    shear = shear - jnp.where(on_left, share(position + 1), 0.0) - jnp.where(on_right, share(EDGE - 1 - position), 0.0)

    tall = (wide, 3 * XW)
    line = lax.broadcasted_iota(jnp.int32, tall, 0)
    column = lax.broadcasted_iota(jnp.int32, tall, 1)
    spread = lax.broadcasted_iota(jnp.int32, (wide, channels), 0) // XW
    spread = (spread == lax.broadcasted_iota(jnp.int32, (wide, channels), 1)).astype(jnp.float32)
    taps = dot(spread, first_ref[...].astype(jnp.float32), exact)
    band = jnp.zeros(tall, jnp.float32)
    for di in range(3):
        for at in range(3):
            hit = (column % XW - line % XW == di - 1) & (column // XW == at)
            band = band + jnp.where(hit, taps[:, 3 * di + at : 3 * di + at + 1], 0.0)

    slab_row = lax.broadcasted_iota(jnp.int32, (wide, TILE), 1) % PACK // angles
    flat_row = lax.broadcasted_iota(jnp.int32, (XW, TILE), 1) % PACK // angles
    mixed = dot(band, shear, exact)
    for r in range(group):
        out_ref[r * wide : (r + 1) * wide, :] = jnp.where(slab_row == r, mixed, 0.0).astype(jnp.bfloat16)
        out_ref[group * wide + r * XW : group * wide + (r + 1) * XW, :] = jnp.where(
            flat_row == r, shear[XW : 2 * XW], 0.0
        ).astype(jnp.bfloat16)

    gather = lax.broadcasted_iota(jnp.int32, (channels, wide), 1) // XW
    gather = (gather == lax.broadcasted_iota(jnp.int32, (channels, wide), 0)).astype(jnp.float32)
    taps = dot(second_ref[...].astype(jnp.float32), gather, exact)
    line = lax.broadcasted_iota(jnp.int32, (XW, wide), 0)
    column = lax.broadcasted_iota(jnp.int32, (XW, wide), 1) % XW
    for at in range(3):
        total = jnp.zeros((XW, wide), jnp.float32)
        for di in range(3):
            total = total + jnp.where(column - line == di - 1, taps[3 * di + at : 3 * di + at + 1, :], 0.0)
        last_ref[at * XW : (at + 1) * XW, :] = total.astype(jnp.bfloat16)


    select_ref[...] = selection(length_ref, select_ref.shape, strip_rows)
    rows = order_ref.shape[0]
    line = lax.broadcasted_iota(jnp.int32, (rows, rows), 0)
    source = lax.broadcasted_iota(jnp.int32, (rows, rows), 1)
    hit = source == line % angles * (rows // angles) + line // angles
    order_ref[...] = jnp.where(hit, 1.0, 0.0).astype(jnp.bfloat16)
    length = length_ref[lax.axis_index("angle")]
    filled_ref[...] = jnp.broadcast_to(length, filled_ref.shape).astype(jnp.float32)


def make_weights(angle_tan, lengths, prior_in, prior_out, strip_rows, parts):
    angles = angle_tan.shape[0]
    channels = prior_in.shape[0]
    rows = PACK // angles * XW * (channels + 1)
    smem = pl.BlockSpec(memory_space=pltpu.SMEM)
    vmem = pl.BlockSpec(memory_space=pltpu.VMEM)
    return pl.pallas_call(
        functools.partial(weights_kernel, strip_rows),
        out_shape=(
            pltpu.VMEM((rows, TILE), jnp.bfloat16),
            pltpu.VMEM((3 * XW, channels * XW), jnp.bfloat16),
            pltpu.VMEM((2 * strip_rows, parts * strip_rows), jnp.bfloat16),
            pltpu.VMEM((2 * strip_rows, 2 * strip_rows), jnp.bfloat16),
            pltpu.VMEM((SUBLANES, LANES), jnp.float32),
        ),
        in_specs=[smem, smem, vmem, vmem],
        out_specs=(vmem,) * 5,
        compiler_params=pltpu.CompilerParams(vmem_limit_bytes=VMEM_LIMIT),
        name="make_weights",
    )(angle_tan, lengths, prior_in.reshape(channels, 9), prior_out.reshape(channels, 9).T)


def slide(values, by, lane):
    if by == 0:
        return values
    width = values.shape[1]
    turned = pltpu.roll(values, (-by) % width, 1)
    return jnp.where((lane < width - by) if by > 0 else (lane >= -by), turned, 0.0)


def volume_kernel(*refs):
    *piece_refs, first_ref, last_ref, order_ref, filled_ref = refs[:-7]
    out_ref, ordered, even, odd, held, blank, sems = refs[-7:]
    angles = len(piece_refs)
    rowcap, width = piece_refs[0].shape
    rows = angles * rowcap
    group = PACK // angles
    groups = rowcap // group
    wide = last_ref.shape[1]
    tiles = width // TILE
    span = 2 * REACH + 1

    ordered[...] = dot(order_ref[...], jnp.concatenate([ref[...] for ref in piece_refs], axis=0))

    lane = lax.broadcasted_iota(jnp.int32, (PACK, width), 1)
    inside = lax.broadcasted_iota(jnp.int32, (PACK, LANES), 1)

    def stack_rows(here, target):
        taken = ordered[pl.ds(pl.multiple_of(here * PACK, PACK), PACK), :]
        moved = {by: slide(taken, by, lane) for by in range(-REACH, REACH + 1)}
        for by, value in moved.items():
            at = (by + REACH) * PACK
            target[at : at + PACK, :] = value.astype(jnp.bfloat16)
        for q in range(EDGE):
            at = (span + q) * PACK
            target[at : at + PACK, :LANES] = jnp.where(inside == 0, moved[q][:, :LANES], 0.0).astype(jnp.bfloat16)
            at += EDGE * PACK
            target[at : at + PACK, width - LANES :] = jnp.where(
                inside == LANES - 1, moved[-q][:, width - LANES :], 0.0
            ).astype(jnp.bfloat16)

    def copy_out(here):
        part = pl.ds(here * group, group)
        return pltpu.make_async_copy(held.at[part], out_ref.at[part], sems.at[here])

    def copy_blank(here):
        return pltpu.make_async_copy(blank, out_ref.at[pl.ds(here * group, group)], sems.at[here])

    def one_group(here, stack):
        base = []
        partial = [[] for _ in range(group)]
        waiting = None
        for n in range(tiles + 1):
            hidden = None
            if n < tiles:
                mixed = dot(first_ref[...], stack[:, n * TILE : (n + 1) * TILE])
                base.append(mixed[group * wide :])
                hidden = jnp.maximum(mixed[: group * wide].astype(jnp.bfloat16), 0.0)
            if waiting is not None:
                for r in range(group):
                    partial[r].append(dot(last_ref[...], waiting[r * wide : (r + 1) * wide]))
            waiting = hidden
        base = jnp.concatenate(base, axis=1)
        for r in range(group):
            sums = jnp.concatenate(partial[r], axis=1)
            held[here * group + r] = (
                base[r * XW : (r + 1) * XW]
                + sums[XW : 2 * XW]
                + slide(sums[:XW], -1, lane)
                + slide(sums[2 * XW :], 1, lane)
            )
        copy_out(here).start()

    even[span * PACK :, :] = jnp.zeros((TILE - span * PACK, width), jnp.bfloat16)
    odd[span * PACK :, :] = jnp.zeros((TILE - span * PACK, width), jnp.bfloat16)
    stack_rows(0, even)

    def two_groups(step, carry):
        here = 2 * step
        stack_rows(here + 1, odd)
        one_group(here, even)
        stack_rows(lax.rem(here + 2, groups), even)
        one_group(here + 1, odd)
        return carry

    filled = jnp.max(filled_ref[...]).astype(jnp.int32)
    pairs = lax.div(filled + 2 * group - 1, 2 * group)
    blank[...] = jnp.zeros_like(blank)

    def skip_group(here, carry):
        copy_blank(here).start()
        return carry

    lax.fori_loop(2 * pairs, groups, skip_group, 0)
    lax.fori_loop(0, pairs, two_groups, 0)

    def finish(here, carry):
        copy_out(here).wait()
        return carry

    lax.fori_loop(0, groups, finish, 0)


def make_volume(pieces, first, last, order, filled):
    angles = len(pieces)
    rowcap, width = pieces[0].shape
    vmem = pl.BlockSpec(memory_space=pltpu.VMEM)
    shape = (rowcap, XW, width)
    return pl.pallas_call(
        volume_kernel,
        out_shape=jax.ShapeDtypeStruct(shape, jnp.float32),
        in_specs=[vmem] * (angles + 4),
        out_specs=pl.BlockSpec(memory_space=pl.ANY),
        scratch_shapes=[
            pltpu.VMEM((angles * rowcap, width), jnp.float32),
            pltpu.VMEM((TILE, width), jnp.bfloat16),
            pltpu.VMEM((TILE, width), jnp.bfloat16),
            pltpu.VMEM(shape, jnp.float32),
            pltpu.VMEM((PACK // angles, XW, width), jnp.float32),
            pltpu.SemaphoreType.DMA((rowcap * angles // PACK,)),
        ],
        compiler_params=pltpu.CompilerParams(vmem_limit_bytes=VMEM_LIMIT),
        name="make_volume",
    )(*pieces, first, last, order, filled)


def body(
    patches,
    magnitudes,
    probe,
    owners,
    scan_rows,
    scan_cols,
    slab_rows,
    angle_tan,
    prior_in,
    prior_out,
):
    tiles = lax.axis_size("tile")
    angles = lax.axis_size("angle")
    half = tiles // 2
    levels = rotate(deal(magnitudes[0], tiles), "tile")
    levels = [levels[step] for step in sending_order(tiles)]
    place = jnp.stack([owners[0, :, 0], scan_rows[0], scan_cols[0]])
    probe, *levels[1:3] = lax.optimization_barrier((probe, *levels[1:3]))
    strips = project(place, *prepare(patches[0], probe), levels)
    near, far = strips[:half], strips[half:]
    angle_tan, prior_in, prior_out, unused = lax.optimization_barrier(
        (angle_tan, prior_in, prior_out, near[0])
    )
    first, last, select, order, filled = make_weights(
        angle_tan, slab_rows[0], prior_in, prior_out, H // tiles, half + 1
    )
    steps = range(half - 1, 0, -1)
    far = [far[0]] + [swap(far[step], "tile", step, tiles) for step in steps]
    far = sum(part.astype(jnp.float32) for part in far).astype(jnp.bfloat16)
    far, *near = lax.optimization_barrier((far, *near))
    far = swap(far, "tile", half, tiles)
    near = [near[0]] + [swap(near[step], "tile", step, tiles) for step in steps]
    select, near[0] = lax.optimization_barrier((select, near[0]))
    slabs = cut_slabs(select, [far] + near, angles)
    return make_volume(rotate(slabs, "angle"), first, last, order, filled)[None]


def solution(mesh):
    placed = (
        P("angle", "tile", None, None, None),
        P("angle", "tile", None, None),
        P(),
        P("angle", "tile", None),
        P("angle", "tile"),
        P("angle", "tile"),
        P("tile", None),
        P(),
        P(),
        P(),
    )
    return jax.shard_map(
        body, mesh=mesh, in_specs=placed, out_specs=P("tile", "angle", None, None), check_vma=False
    )
```

```python
import functools

import jax
import jax.numpy as jnp
import numpy as np
from jax import lax
from jax.experimental import pallas as pl
from jax.experimental.pallas import tpu as pltpu
from jax.sharding import PartitionSpec as P

H = 512
W = 1024
XW = 16
LANES = 128
SUBLANES = 8
PACK = 16
BEND = 3
REACH = BEND + 1
EDGE = BEND
TILE = 256
PAIR = 4
VMEM_LIMIT = 24 * 1024 * 1024


def dft_table(side):
    index = np.arange(side)
    phase = (index[:, None] * index[None, :] % side).astype(np.float64) * (2.0 * np.pi / side)
    scale = 1.0 / np.sqrt(side)
    real = np.cos(phase) * scale
    imag = -np.sin(phase) * scale
    table = np.block([[real, imag], [-imag, real]]).astype(np.float32)
    return jnp.asarray(table.astype(jnp.bfloat16))


def dot(left, right, precision=None):
    return jnp.dot(left, right, preferred_element_type=jnp.float32, precision=precision)


def swap_halves(values, pair, side):
    return jnp.concatenate(
        [
            jnp.concatenate(
                [values[k * side : (k + 1) * side, h * side : (h + 1) * side] for k in range(pair)], axis=1
            )
            for h in range(2)
        ],
        axis=0,
    )


def ahead(axis, step, size):
    return lax.rem(lax.axis_index(axis) + step, size)


def behind(axis, step, size):
    return lax.rem(lax.axis_index(axis) + (size - step), size)


def sending_orders(size):
    light = sorted(range(1, size), key=lambda step: (-abs(2 * step - size), step))
    heavy = sorted(range(1, size), key=lambda step: (abs(2 * step - size), step))
    return [0] + heavy, [0] + light


def step_at(position, size):
    even, odd = sending_orders(size)
    return jnp.where(lax.rem(lax.axis_index("angle"), 2) == 0, even[position], odd[position])


def rotate(values, axis):
    size = len(values)
    return [values[0]] + [
        lax.ppermute(values[step], axis, [(a, (a + step) % size) for a in range(size)])
        for step in range(1, size)
    ]


def swap(value, axis, step, size):
    return lax.ppermute(value, axis, [(a, a ^ step) for a in range(size)])


def deal_kernel(frames_ref, *refs):
    *out_refs, sems = refs
    tiles = len(out_refs)
    depth = out_refs[0].shape[0]
    copies = [
        pltpu.make_async_copy(
            frames_ref.at[pl.ds(ahead("tile", step_at(k, tiles), tiles) * depth, depth)], out_refs[k], sems.at[k]
        )
        for k in range(tiles)
    ]
    for copy in copies:
        copy.start()
    for copy in copies:
        copy.wait()


def deal(frames, tiles):
    depth = frames.shape[0] // tiles
    return pl.pallas_call(
        deal_kernel,
        out_shape=(jax.ShapeDtypeStruct((depth,) + frames.shape[1:], frames.dtype),) * tiles,
        in_specs=[pl.BlockSpec(memory_space=pltpu.HBM)],
        out_specs=(pl.BlockSpec(memory_space=pltpu.VMEM),) * tiles,
        scratch_shapes=[pltpu.SemaphoreType.DMA((tiles,))],
        compiler_params=pltpu.CompilerParams(vmem_limit_bytes=VMEM_LIMIT),
        name="deal",
    )(pltpu.with_memory_space_constraint(frames, pltpu.HBM))


def turned_table(table):
    side = table.shape[0] // 2
    return jnp.concatenate(
        [
            jnp.concatenate([table[:side, :side], table[side:, :side]], axis=1),
            jnp.concatenate([table[:side, side:], table[side:, side:]], axis=1),
        ],
        axis=0,
    )


def prepare_kernel(patch_hbm, probe_hbm, table_hbm, unit_ref, probe_ref, table_ref, patch_ref, sems):
    count, _, side, _ = patch_ref.shape
    steps = count // PAIR
    small = [
        pltpu.make_async_copy(source, target, sems.at[steps + k])
        for k, (source, target) in enumerate(((table_hbm, table_ref), (probe_hbm, probe_ref)))
    ]
    large = [
        pltpu.make_async_copy(
            patch_hbm.at[pl.ds(k * PAIR, PAIR)], patch_ref.at[pl.ds(k * PAIR, PAIR)], sems.at[k]
        )
        for k in range(steps)
    ]
    for copy in small[:1] + large + small[1:]:
        copy.start()
    small[0].wait()
    table = table_ref[...]
    left = turned_table(table)
    for step in range(steps):
        large[step].wait()
        first = step * PAIR
        joined = jnp.concatenate(
            [jnp.concatenate([patch_ref[k, 0], patch_ref[k, 1]], axis=1) for k in range(first, first + PAIR)],
            axis=0,
        )
        half = dot(joined, table).astype(jnp.bfloat16)
        spectrum = dot(left, swap_halves(half, PAIR, side))
        real = spectrum[:side]
        imag = spectrum[side:]
        factor = lax.rsqrt(real * real + imag * imag + 0.25)
        cut = slice(first * side, (first + PAIR) * side)
        unit_ref[:side, cut] = real * factor
        unit_ref[side:, cut] = imag * factor
    small[1].wait()


def prepare(waves, probe):
    count, _, side, _ = waves.shape
    hbm = pl.BlockSpec(memory_space=pltpu.HBM)
    vmem = pl.BlockSpec(memory_space=pltpu.VMEM)
    return pl.pallas_call(
        prepare_kernel,
        out_shape=(
            pltpu.VMEM((2 * side, count * side), jnp.float32),
            pltpu.VMEM(probe.shape, jnp.float32),
            pltpu.VMEM((2 * side, 2 * side), jnp.bfloat16),
        ),
        in_specs=[hbm] * 3,
        out_specs=(vmem,) * 3,
        scratch_shapes=[
            pltpu.VMEM(waves.shape, waves.dtype),
            pltpu.SemaphoreType.DMA((count // PAIR + 2,)),
        ],
        compiler_params=pltpu.CompilerParams(vmem_limit_bytes=VMEM_LIMIT),
        name="prepare",
    )(*[pltpu.with_memory_space_constraint(x, pltpu.HBM) for x in (waves, probe, dft_table(side))])


def project_kernel(tiles, place_ref, unit_ref, probe_ref, table_ref, *refs):
    level_refs, out_refs = refs[:tiles], refs[tiles : 2 * tiles]
    canvas, levels = refs[2 * tiles :]
    depth, side = level_refs[0].shape[:2]
    count = unit_ref.shape[1] // side
    for step, level_ref in enumerate(level_refs):
        levels[step * depth : (step + 1) * depth] = level_ref[...]
    owner = [place_ref[0, k] for k in range(count)]
    slots = []
    for k in range(count):
        rank = jnp.int32(0)
        for j in range(k):
            rank = rank + jnp.where(owner[j] == owner[k], 1, 0)
        step = behind("tile", owner[k], tiles)
        slot = rank
        for at in range(1, tiles):
            slot = slot + jnp.where(step == step_at(at, tiles), at * depth, 0)
        slots.append(slot)
    table = table_ref[...]
    left = turned_table(table)
    canvas[...] = jnp.zeros_like(canvas)
    tall = side + SUBLANES
    lane = lax.broadcasted_iota(jnp.int32, (tall, side), 1)
    for first in range(0, count, PAIR):
        level = [levels[slots[k]].astype(jnp.float32) for k in range(first, first + PAIR)]
        level = jnp.concatenate(level, axis=1)
        cut = slice(first * side, (first + PAIR) * side)
        real = (unit_ref[:side, cut] * level).astype(jnp.bfloat16)
        imag = (unit_ref[side:, cut] * level).astype(jnp.bfloat16)
        target = jnp.concatenate(
            [
                jnp.concatenate([real[:, k * side : (k + 1) * side], imag[:, k * side : (k + 1) * side]], axis=1)
                for k in range(PAIR)
            ],
            axis=0,
        )
        back = dot(target, left).astype(jnp.bfloat16)
        result = dot(table, swap_halves(back, PAIR, side))
        for k in range(PAIR):
            fixed_re = result[:side, k * side : (k + 1) * side]
            fixed_im = result[side:, k * side : (k + 1) * side]
            contrib = probe_ref[0] * fixed_im - probe_ref[1] * fixed_re
            row = place_ref[1, first + k]
            col = place_ref[2, first + k]
            down = lax.rem(row, SUBLANES)
            shift = lax.rem(col, LANES)
            top = pl.multiple_of(row - down, SUBLANES)
            base = pl.multiple_of(col - shift, LANES)
            turned = jnp.concatenate([contrib, jnp.zeros((SUBLANES, side), jnp.float32)], axis=0)
            turned = pltpu.roll(pltpu.roll(turned, down, 0), shift, 1)
            piece = jnp.concatenate(
                [jnp.where(lane >= shift, turned, 0.0), jnp.where(lane < shift, turned, 0.0)], axis=1
            )
            where = (pl.ds(top, tall), pl.ds(base, 2 * side))
            canvas[where] = canvas[where] + piece
    strip_rows, width = out_refs[0].shape
    me = lax.axis_index("tile")
    for step in range(tiles):
        top = pl.multiple_of(lax.bitwise_xor(me, jnp.int32(step)) * strip_rows, strip_rows)
        out_refs[step][...] = canvas[pl.ds(top, strip_rows), :width].astype(jnp.bfloat16)


def project(place, unit, probe, table, levels):
    tiles = len(levels)
    depth, side = levels[0].shape[:2]
    smem = pl.BlockSpec(memory_space=pltpu.SMEM)
    vmem = pl.BlockSpec(memory_space=pltpu.VMEM)
    return pl.pallas_call(
        functools.partial(project_kernel, tiles),
        out_shape=(jax.ShapeDtypeStruct((H // tiles, W), jnp.bfloat16),) * tiles,
        in_specs=[smem] + [vmem] * (3 + tiles),
        out_specs=(vmem,) * tiles,
        scratch_shapes=[
            pltpu.VMEM((H + SUBLANES, W + side), jnp.float32),
            pltpu.VMEM((tiles * depth, side, side), levels[0].dtype),
        ],
        compiler_params=pltpu.CompilerParams(vmem_limit_bytes=VMEM_LIMIT),
        name="project",
    )(place, unit, probe, table, *levels)


def slabs_kernel(count, select_ref, *refs):
    strips = jnp.concatenate([ref[...] for ref in refs[:count]], axis=0)
    result = dot(select_ref[...], strips).astype(jnp.bfloat16)
    rowcap = refs[count].shape[0]
    for step, out_ref in enumerate(refs[count:]):
        out_ref[...] = result[step * rowcap : (step + 1) * rowcap]


def cut_slabs(select, strips, angles):
    rowcap = select.shape[0] // angles
    vmem = pl.BlockSpec(memory_space=pltpu.VMEM)
    return pl.pallas_call(
        functools.partial(slabs_kernel, len(strips)),
        out_shape=(jax.ShapeDtypeStruct((rowcap, strips[0].shape[1]), jnp.bfloat16),) * angles,
        in_specs=[vmem] * (1 + len(strips)),
        out_specs=(vmem,) * angles,
        compiler_params=pltpu.CompilerParams(vmem_limit_bytes=VMEM_LIMIT),
        name="cut_slabs",
    )(select, *strips)


def selection(length_ref, shape, strip_rows):
    angles = length_ref.shape[0]
    rowcap = shape[0] // angles
    row = lax.broadcasted_iota(jnp.int32, shape, 0)
    source = lax.broadcasted_iota(jnp.int32, shape, 1) % strip_rows
    wanted = jnp.full(shape, -1, jnp.int32)
    for step in range(angles):
        slab = ahead("angle", step, angles)
        start = jnp.int32(0)
        for q in range(angles):
            start = start + jnp.where(q < slab, length_ref[q], 0)
        within = row - step * rowcap
        good = (within >= 0) & (within < rowcap) & (within < length_ref[slab])
        wanted = jnp.where(good, within + start, wanted)
    return jnp.where(source == wanted, 1.0, 0.0).astype(jnp.bfloat16)


def weights_kernel(strip_rows, tan_ref, length_ref, first_ref, second_ref, out_ref, last_ref, select_ref, order_ref, filled_ref):
    angles = tan_ref.shape[0]
    channels = first_ref.shape[0]
    group = PACK // angles
    wide = channels * XW
    steps = 2 * REACH + 1
    exact = lax.Precision.HIGHEST

    shape = (3 * XW, TILE)
    line = lax.broadcasted_iota(jnp.int32, shape, 0)
    column = lax.broadcasted_iota(jnp.int32, shape, 1)
    dj = line // XW - 1
    offset = (line % XW).astype(jnp.float32) - (XW - 1) / 2.0
    step = column // PACK
    tangent = jnp.zeros(shape, jnp.float32)
    for a in range(angles):
        source = behind("angle", a, angles)
        tangent = jnp.where(column % angles == a, tan_ref[source], tangent)
    shifted = jnp.clip(offset * tangent, -float(BEND), float(BEND))
    floor_shift = jnp.floor(shifted)
    fraction = shifted - floor_shift

    def share(at):
        at = at.astype(jnp.float32)
        low = jnp.where(at == floor_shift, 1.0 - fraction, 0.0)
        return (low + jnp.where(at == floor_shift + 1.0, fraction, 0.0)) * (0.25 / angles)

    position = step - steps
    shear = jnp.where(step < steps, share(step - REACH - dj), 0.0)
    on_left = (position >= 0) & (position < EDGE) & (dj == -1)
    on_right = (position >= EDGE) & (position < 2 * EDGE) & (dj == 1)
    shear = shear - jnp.where(on_left, share(position + 1), 0.0) - jnp.where(on_right, share(EDGE - 1 - position), 0.0)

    tall = (wide, 3 * XW)
    line = lax.broadcasted_iota(jnp.int32, tall, 0)
    column = lax.broadcasted_iota(jnp.int32, tall, 1)
    spread = lax.broadcasted_iota(jnp.int32, (wide, channels), 0) // XW
    spread = (spread == lax.broadcasted_iota(jnp.int32, (wide, channels), 1)).astype(jnp.float32)
    taps = dot(spread, first_ref[...].astype(jnp.float32), exact)
    band = jnp.zeros(tall, jnp.float32)
    for di in range(3):
        for at in range(3):
            hit = (column % XW - line % XW == di - 1) & (column // XW == at)
            band = band + jnp.where(hit, taps[:, 3 * di + at : 3 * di + at + 1], 0.0)

    slab_row = lax.broadcasted_iota(jnp.int32, (wide, TILE), 1) % PACK // angles
    flat_row = lax.broadcasted_iota(jnp.int32, (XW, TILE), 1) % PACK // angles
    mixed = dot(band, shear, exact)
    for r in range(group):
        out_ref[r * wide : (r + 1) * wide, :] = jnp.where(slab_row == r, mixed, 0.0).astype(jnp.bfloat16)
        out_ref[group * wide + r * XW : group * wide + (r + 1) * XW, :] = jnp.where(
            flat_row == r, shear[XW : 2 * XW], 0.0
        ).astype(jnp.bfloat16)

    gather = lax.broadcasted_iota(jnp.int32, (channels, wide), 1) // XW
    gather = (gather == lax.broadcasted_iota(jnp.int32, (channels, wide), 0)).astype(jnp.float32)
    taps = dot(second_ref[...].astype(jnp.float32), gather, exact)
    line = lax.broadcasted_iota(jnp.int32, (XW, wide), 0)
    column = lax.broadcasted_iota(jnp.int32, (XW, wide), 1) % XW
    for at in range(3):
        total = jnp.zeros((XW, wide), jnp.float32)
        for di in range(3):
            total = total + jnp.where(column - line == di - 1, taps[3 * di + at : 3 * di + at + 1, :], 0.0)
        last_ref[at * XW : (at + 1) * XW, :] = total.astype(jnp.bfloat16)


    select_ref[...] = selection(length_ref, select_ref.shape, strip_rows)
    rows = order_ref.shape[0]
    line = lax.broadcasted_iota(jnp.int32, (rows, rows), 0)
    source = lax.broadcasted_iota(jnp.int32, (rows, rows), 1)
    hit = source == line % angles * (rows // angles) + line // angles
    order_ref[...] = jnp.where(hit, 1.0, 0.0).astype(jnp.bfloat16)
    length = length_ref[lax.axis_index("angle")]
    filled_ref[...] = jnp.broadcast_to(length, filled_ref.shape).astype(jnp.float32)


def make_weights(angle_tan, lengths, prior_in, prior_out, strip_rows, parts):
    angles = angle_tan.shape[0]
    channels = prior_in.shape[0]
    rows = PACK // angles * XW * (channels + 1)
    smem = pl.BlockSpec(memory_space=pltpu.SMEM)
    vmem = pl.BlockSpec(memory_space=pltpu.VMEM)
    return pl.pallas_call(
        functools.partial(weights_kernel, strip_rows),
        out_shape=(
            pltpu.VMEM((rows, TILE), jnp.bfloat16),
            pltpu.VMEM((3 * XW, channels * XW), jnp.bfloat16),
            pltpu.VMEM((2 * strip_rows, parts * strip_rows), jnp.bfloat16),
            pltpu.VMEM((2 * strip_rows, 2 * strip_rows), jnp.bfloat16),
            pltpu.VMEM((SUBLANES, LANES), jnp.float32),
        ),
        in_specs=[smem, smem, vmem, vmem],
        out_specs=(vmem,) * 5,
        compiler_params=pltpu.CompilerParams(vmem_limit_bytes=VMEM_LIMIT),
        name="make_weights",
    )(angle_tan, lengths, prior_in.reshape(channels, 9), prior_out.reshape(channels, 9).T)


def slide(values, by, lane):
    if by == 0:
        return values
    width = values.shape[1]
    turned = pltpu.roll(values, (-by) % width, 1)
    return jnp.where((lane < width - by) if by > 0 else (lane >= -by), turned, 0.0)


def volume_kernel(*refs):
    *piece_refs, first_ref, last_ref, order_ref, filled_ref = refs[:-7]
    out_ref, ordered, even, odd, held, blank, sems = refs[-7:]
    angles = len(piece_refs)
    rowcap, width = piece_refs[0].shape
    rows = angles * rowcap
    group = PACK // angles
    groups = rowcap // group
    wide = last_ref.shape[1]
    tiles = width // TILE
    span = 2 * REACH + 1

    ordered[...] = dot(order_ref[...], jnp.concatenate([ref[...] for ref in piece_refs], axis=0))

    lane = lax.broadcasted_iota(jnp.int32, (PACK, width), 1)
    inside = lax.broadcasted_iota(jnp.int32, (PACK, LANES), 1)

    def stack_rows(here, target):
        taken = ordered[pl.ds(pl.multiple_of(here * PACK, PACK), PACK), :]
        moved = {by: slide(taken, by, lane) for by in range(-REACH, REACH + 1)}
        for by, value in moved.items():
            at = (by + REACH) * PACK
            target[at : at + PACK, :] = value.astype(jnp.bfloat16)
        for q in range(EDGE):
            at = (span + q) * PACK
            target[at : at + PACK, :LANES] = jnp.where(inside == 0, moved[q][:, :LANES], 0.0).astype(jnp.bfloat16)
            at += EDGE * PACK
            target[at : at + PACK, width - LANES :] = jnp.where(
                inside == LANES - 1, moved[-q][:, width - LANES :], 0.0
            ).astype(jnp.bfloat16)

    def copy_out(here):
        part = pl.ds(here * group, group)
        return pltpu.make_async_copy(held.at[part], out_ref.at[part], sems.at[here])

    def copy_blank(here):
        return pltpu.make_async_copy(blank, out_ref.at[pl.ds(here * group, group)], sems.at[here])

    def one_group(here, stack):
        base = []
        partial = [[] for _ in range(group)]
        waiting = None
        for n in range(tiles + 1):
            hidden = None
            if n < tiles:
                mixed = dot(first_ref[...], stack[:, n * TILE : (n + 1) * TILE])
                base.append(mixed[group * wide :])
                hidden = jnp.maximum(mixed[: group * wide].astype(jnp.bfloat16), 0.0)
            if waiting is not None:
                for r in range(group):
                    partial[r].append(dot(last_ref[...], waiting[r * wide : (r + 1) * wide]))
            waiting = hidden
        base = jnp.concatenate(base, axis=1)
        for r in range(group):
            sums = jnp.concatenate(partial[r], axis=1)
            held[here * group + r] = (
                base[r * XW : (r + 1) * XW]
                + sums[XW : 2 * XW]
                + slide(sums[:XW], -1, lane)
                + slide(sums[2 * XW :], 1, lane)
            )
        copy_out(here).start()

    even[span * PACK :, :] = jnp.zeros((TILE - span * PACK, width), jnp.bfloat16)
    odd[span * PACK :, :] = jnp.zeros((TILE - span * PACK, width), jnp.bfloat16)
    stack_rows(0, even)

    def two_groups(step, carry):
        here = 2 * step
        stack_rows(here + 1, odd)
        one_group(here, even)
        stack_rows(lax.rem(here + 2, groups), even)
        one_group(here + 1, odd)
        return carry

    filled = jnp.max(filled_ref[...]).astype(jnp.int32)
    pairs = lax.div(filled + 2 * group - 1, 2 * group)
    blank[...] = jnp.zeros_like(blank)

    def skip_group(here, carry):
        copy_blank(here).start()
        return carry

    lax.fori_loop(2 * pairs, groups, skip_group, 0)
    lax.fori_loop(0, pairs, two_groups, 0)

    def finish(here, carry):
        copy_out(here).wait()
        return carry

    lax.fori_loop(0, groups, finish, 0)


def make_volume(pieces, first, last, order, filled):
    angles = len(pieces)
    rowcap, width = pieces[0].shape
    vmem = pl.BlockSpec(memory_space=pltpu.VMEM)
    shape = (rowcap, XW, width)
    return pl.pallas_call(
        volume_kernel,
        out_shape=jax.ShapeDtypeStruct(shape, jnp.float32),
        in_specs=[vmem] * (angles + 4),
        out_specs=pl.BlockSpec(memory_space=pl.ANY),
        scratch_shapes=[
            pltpu.VMEM((angles * rowcap, width), jnp.float32),
            pltpu.VMEM((TILE, width), jnp.bfloat16),
            pltpu.VMEM((TILE, width), jnp.bfloat16),
            pltpu.VMEM(shape, jnp.float32),
            pltpu.VMEM((PACK // angles, XW, width), jnp.float32),
            pltpu.SemaphoreType.DMA((rowcap * angles // PACK,)),
        ],
        compiler_params=pltpu.CompilerParams(vmem_limit_bytes=VMEM_LIMIT),
        name="make_volume",
    )(*pieces, first, last, order, filled)


def body(
    patches,
    magnitudes,
    probe,
    owners,
    scan_rows,
    scan_cols,
    slab_rows,
    angle_tan,
    prior_in,
    prior_out,
):
    tiles = lax.axis_size("tile")
    angles = lax.axis_size("angle")
    half = tiles // 2
    orders = sending_orders(tiles)
    levels = deal(magnitudes[0], tiles)
    levels = [levels[0]] + [
        lax.ppermute(
            levels[k],
            ("angle", "tile"),
            [
                (a * tiles + t, a * tiles + (t + orders[a % 2][k]) % tiles)
                for a in range(angles)
                for t in range(tiles)
            ],
        )
        for k in range(1, tiles)
    ]
    place = jnp.stack([owners[0, :, 0], scan_rows[0], scan_cols[0]])
    probe, *levels[1:3] = lax.optimization_barrier((probe, *levels[1:3]))
    strips = project(place, *prepare(patches[0], probe), levels)
    near, far = strips[:half], strips[half:]
    angle_tan, prior_in, prior_out, unused = lax.optimization_barrier(
        (angle_tan, prior_in, prior_out, near[0])
    )
    first, last, select, order, filled = make_weights(
        angle_tan, slab_rows[0], prior_in, prior_out, H // tiles, half + 1
    )
    steps = range(half - 1, 0, -1)
    far = [far[0]] + [swap(far[step], "tile", step, tiles) for step in steps]
    far = sum(part.astype(jnp.float32) for part in far).astype(jnp.bfloat16)
    far, *near = lax.optimization_barrier((far, *near))
    far = swap(far, "tile", half, tiles)
    near = [near[0]] + [swap(near[step], "tile", step, tiles) for step in steps]
    select, near[0] = lax.optimization_barrier((select, near[0]))
    slabs = cut_slabs(select, [far] + near, angles)
    return make_volume(rotate(slabs, "angle"), first, last, order, filled)[None]


def solution(mesh):
    placed = (
        P("angle", "tile", None, None, None),
        P("angle", "tile", None, None),
        P(),
        P("angle", "tile", None),
        P("angle", "tile"),
        P("angle", "tile"),
        P("tile", None),
        P(),
        P(),
        P(),
    )
    return jax.shard_map(
        body, mesh=mesh, in_specs=placed, out_specs=P("tile", "angle", None, None), check_vma=False
    )
```
